32 devices in a mesh: section: 4 (over y, x), row: 4 (over z), col: 2 (over core).
Axes of the slice: x: 2, y: 2, z: 4, core: 2. Of those that a mesh axis runs over, the one named last changes fastest.
Arguments:
- hidden: bfloat16 [4, 256, 2, 3072], P(None, ('row', 'col')), may hold values from -6 to 6
- patch_counts: int32 [2, 4], replicated, may hold values from 128 to 256, as said below
- timestep: int32 [1], replicated, may hold values from 0 to 999
- time_table: float32 [1000, 512], replicated, may hold values from -6 to 6
- ada_weight: bfloat16 [4, 512, 18432], P('section', None, ('row', 'col')), may hold values from -0.25 to 0.25
- qkv_weight: bfloat16 [4, 3072, 9216], P('section', None, 'col'), may hold values from -0.109375 to 0.109375
- out_weight: bfloat16 [4, 3072, 3072], P('section', 'col'), may hold values from -0.109375 to 0.109375
- qk_gain: float32 [4, 2, 64], P('section'), may hold values from 1 to 3
- stale_kv: bfloat16 [4, 1024, 2, 48, 128], P('section', None, None, 'col'), may hold values from -8 to 8
- stale_inputs: bfloat16 [4, 96, 2, 3072], P('section', ('row', 'col')), may hold values from -6 to 6
- recompute_slots: int32 [2, 96], replicated, may hold values from 0 to 1023, as said below
Outputs:
- layer_outputs: bfloat16 [4, 4, 256, 2, 3072], P('section', None, ('row', 'col'))
The draws below stay inside these ranges and needn't reach their ends.
Inputs may be any that keep to these rules, and one draw needn't show every extreme that they name: `patch_counts`: in every request one patch holds exactly 256 live tokens and another exactly 128. `recompute_slots`: the slots of one request are distinct.
All inputs are finite; a program needn't handle non-finite values.
Results may differ from the reference program's by a relative error of at most 0.035.
Values may be sent and summed in bfloat16 or wider, within the bound.
A program may use at most 192 MiB of HBM per device.

```python
import math
import jax
import jax.numpy as jnp
from jax import lax

HEADS = 48
HD = 64
D = 3072
TEMB = 512
TXT = 226
STEPS = 1000
GH = 30
GW = 45
REQS = 2
PATCHES = 4
PLEN = 256
LEN = 1024
HPC = 24
REC = 96
N_SECTION = 4
N_COL = 2


def draw_patch_counts(key, part):
    counts = jax.random.randint(key, (REQS, PATCHES), PLEN // 2, PLEN + 1)
    full_patch = jax.random.randint(jax.random.fold_in(key, 7), (REQS,), 0, PATCHES)
    short_patch = (full_patch + 1) % PATCHES
    patch_ids = jnp.arange(PATCHES)[None, :]
    counts = jnp.where(patch_ids == full_patch[:, None], PLEN, counts)
    counts = jnp.where(patch_ids == short_patch[:, None], PLEN // 2, counts)
    return counts.astype(jnp.int32)


def draw_recompute_slots(key, part):
    keys_all = jax.random.split(key, REQS)

    def pick_slots(one_key):
        return jax.random.permutation(one_key, LEN)[:REC].astype(jnp.int32)
    return jax.vmap(pick_slots)(keys_all)


def block_scale(stream_key, extent, shards, least, top_value):
    def one(position, parts):
        draws = jax.random.uniform(jax.random.fold_in(jax.random.fold_in(stream_key, 6), position), (parts,), jnp.float32, least / len(shards), top_value / len(shards))
        return jnp.repeat(jnp.exp(draws), extent[position] // parts).reshape((-1,) + (1,) * (len(extent) - position - 1))

    level = one(*shards[0])
    for cut in shards[1:]:
        level = level * one(*cut)
    return level


def bell_draw(stream_key, shape, deviation, reach, shards=(), held_as=jnp.bfloat16):
    values = jax.random.normal(stream_key, shape, jnp.float32) * deviation
    if len(shards) > 0:
        values = block_scale(stream_key, shape, shards, -0.22, 0.18) * values
    return jnp.clip(values, min=-reach, max=reach).astype(held_as)


def setup_inputs(seed: int = 0) -> dict:
    key_list = jax.random.split(jax.random.key(seed), 12)
    hidden = bell_draw(key_list[0], (PATCHES, PLEN, REQS, D), 1.0, 6.0, ((1, 8),))
    patch_counts = draw_patch_counts(jax.random.fold_in(key_list[11], 71), 0)
    timestep = jax.random.randint(key_list[2], (1,), 0, STEPS).astype(jnp.int32)
    time_table = bell_draw(key_list[3], (STEPS, TEMB), 1.0, 6.0, (), jnp.float32)
    ada_weight = bell_draw(key_list[4], (N_SECTION, TEMB, 6 * D), TEMB ** -0.5, 0.25, ((0, 4), (2, 8)))
    qkv_weight = bell_draw(key_list[5], (N_SECTION, D, 3 * D), D ** -0.5, 0.109375, ((0, 4), (2, 2)))
    out_weight = bell_draw(key_list[6], (N_SECTION, D, D), D ** -0.5, 0.109375, ((0, 4), (1, 2)))
    qk_gain = jnp.clip(jnp.exp(math.log(3.0) - 1.0986123 * jax.random.uniform(key_list[7], (N_SECTION, 2, HD), jnp.float32) ** block_scale(key_list[7], (N_SECTION, 2, HD), ((0, 4),), -0.2, 0.2)), 1.0, 3.0)
    stale_kv = bell_draw(key_list[8], (N_SECTION, LEN, REQS, HEADS, 2 * HD), 1.5, 8.0, ((0, 4), (3, 2)))
    stale_inputs = bell_draw(key_list[9], (N_SECTION, REC, REQS, D), 1.0, 6.0, ((0, 4), (1, 8)))
    recompute_slots = draw_recompute_slots(jax.random.fold_in(key_list[11], 71), 0)
    return {"hidden": hidden, "patch_counts": patch_counts, "timestep": timestep, "time_table": time_table, "ada_weight": ada_weight, "qkv_weight": qkv_weight, "out_weight": out_weight, "qk_gain": qk_gain, "stale_kv": stale_kv, "stale_inputs": stale_inputs, "recompute_slots": recompute_slots}


def layer_norm(values, epsilon):
    centered = values - lax.optimization_barrier(jnp.mean(values, axis=-1, keepdims=True))
    return centered * lax.rsqrt(lax.optimization_barrier(jnp.mean(centered * centered, axis=-1, keepdims=True)) + epsilon)

def rotary_tables(positions):
    video_index = jnp.maximum(positions - TXT, 0)
    is_video = positions >= TXT
    frame_index = video_index // (GH * GW)
    height_index = video_index // GW % GH
    width_index = video_index % GW
    phase_parts = []
    for coordinate, part_size in ((frame_index, HD // 4), (height_index, HD * 3 // 8), (width_index, HD * 3 // 8)):
        frequency = 1.0 / 10000.0 ** (jnp.arange(0, part_size, 2).astype(jnp.float32) / part_size)
        phase_part = coordinate.astype(jnp.float32)[..., None] * frequency
        phase_parts.append(jnp.repeat(phase_part, 2, axis=-1))
    phase_all = jnp.concatenate(phase_parts, axis=-1)
    cosine = jnp.where(is_video[..., None], jnp.cos(phase_all), 1.0)
    sine_table = jnp.where(is_video[..., None], jnp.sin(phase_all), 0.0)
    return (cosine, sine_table)

def rotate_pairs(values, cosine, sine_table):
    paired = values.reshape(values.shape[:-1] + (values.shape[-1] // 2, 2))
    turned = jnp.stack([-paired[..., 1], paired[..., 0]], axis=-1).reshape(values.shape)
    return values * cosine + turned * sine_table

def heads_from(mixed_rows, positions, gain_pair, with_queries):
    cosine, sine_table = rotary_tables(positions)
    cosine = cosine[..., None, :]
    sine_table = sine_table[..., None, :]
    keys_new = rotate_pairs(layer_norm(mixed_rows[..., 1, :], 1e-06) * gain_pair[1], cosine, sine_table).astype(jnp.bfloat16)
    values_new = mixed_rows[..., 2, :].astype(jnp.bfloat16)
    key_value = jnp.concatenate([keys_new, values_new], axis=-1)
    if with_queries:
        queries = rotate_pairs(layer_norm(mixed_rows[..., 0, :], 1e-06) * gain_pair[0], cosine, sine_table).astype(jnp.bfloat16)
        return (queries, key_value)
    return key_value

def modulate(row_values, positions, modulation):
    is_text = (positions < TXT)[..., None]
    shifts = jnp.where(is_text, modulation[3], modulation[0])
    scales = jnp.where(is_text, modulation[4], modulation[1])
    normed = layer_norm(row_values.astype(jnp.float32), 1e-05)
    return (normed * (1.0 + scales) + shifts).astype(jnp.bfloat16)

def reference(hidden, patch_counts, timestep, time_table, ada_weight, qkv_weight, out_weight, qk_gain, stale_kv, stale_inputs, recompute_slots):
    starts = jnp.cumsum(patch_counts, axis=1) - patch_counts
    slot_index = jnp.arange(LEN, dtype=jnp.int32)
    slot_patch = slot_index // PLEN
    slot_offset = slot_index % PLEN
    positions = starts[:, slot_patch] + slot_offset[None, :]
    live_mask = slot_offset[None, :] < patch_counts[:, slot_patch]
    slot_positions = positions.T
    embedding = jax.nn.silu(time_table[timestep[0]]).astype(jnp.bfloat16)
    scale_factor = HD ** (-0.5)
    current = hidden
    results = []
    for layer_index in range(N_SECTION):
        modulation = jnp.dot(embedding, ada_weight[layer_index], preferred_element_type=jnp.float32).reshape(6, D)
        slot_rows = current.reshape(LEN, REQS, D)
        normed = modulate(slot_rows, slot_positions, modulation)
        mixed_rows = jnp.dot(normed.reshape(LEN * REQS, D), qkv_weight[layer_index], preferred_element_type=jnp.float32)
        queries, fresh_pairs = heads_from(mixed_rows.reshape(LEN, REQS, HEADS, 3, HD), slot_positions, qk_gain[layer_index], True)
        rec_positions = jnp.take_along_axis(positions, recompute_slots, axis=1).T
        rec_normed = modulate(stale_inputs[layer_index], rec_positions, modulation)
        rec_mixed = jnp.dot(rec_normed.reshape(REC * REQS, D), qkv_weight[layer_index], preferred_element_type=jnp.float32)
        rec_pairs = heads_from(rec_mixed.reshape(REC, REQS, HEADS, 3, HD), rec_positions, qk_gain[layer_index], False)
        base_cache = stale_kv[layer_index]
        for request in range(REQS):
            base_cache = base_cache.at[recompute_slots[request], request].set(rec_pairs[:, request])
        patch_outputs = []
        for patch_index in range(PATCHES):
            use_fresh = (slot_patch <= patch_index)[:, None, None, None]
            cache_table = jnp.where(use_fresh, fresh_pairs, base_cache)
            patch_queries = queries[patch_index * PLEN:(patch_index + 1) * PLEN]
            scores = jnp.einsum('qrhd,krhd->rhqk', patch_queries.astype(jnp.float32), cache_table[..., :HD].astype(jnp.float32)) * scale_factor
            weights = jnp.where(live_mask[:, None, None, :], jnp.exp(scores), 0.0)
            totals = lax.optimization_barrier(jnp.sum(weights, axis=-1))
            rounded = lax.optimization_barrier(weights.astype(jnp.bfloat16)).astype(jnp.float32)
            attended = jnp.einsum('rhqk,krhd->qrhd', rounded, cache_table[..., HD:].astype(jnp.float32))
            attended = (attended / jnp.transpose(totals, (2, 0, 1))[..., None]).astype(jnp.bfloat16)
            grouped = lax.optimization_barrier(attended).reshape(PLEN * REQS, N_COL, HPC * HD).astype(jnp.float32)
            weight_groups = out_weight[layer_index].reshape(N_COL, HPC * HD, D).astype(jnp.float32)
            partials = jnp.einsum('ngc,gcd->gnd', grouped, weight_groups)
            partials = lax.optimization_barrier(partials.astype(jnp.bfloat16)).astype(jnp.float32)
            projected = lax.optimization_barrier(jnp.sum(partials, axis=0)).reshape(PLEN, REQS, D)
            patch_positions = slot_positions[patch_index * PLEN:(patch_index + 1) * PLEN]
            is_text = (patch_positions < TXT)[..., None]
            gate_rows = jnp.where(is_text, modulation[5], modulation[2])
            old_rows = current[patch_index].astype(jnp.float32)
            patch_outputs.append((old_rows + gate_rows * projected).astype(jnp.bfloat16))
        current = jnp.stack(patch_outputs, axis=0)
        results.append(current)
    return jnp.stack(results, axis=0)
```

```python
import jax
import jax.numpy as jnp
from jax import lax
from jax.experimental import pallas as pl
from jax.experimental.pallas import tpu as pltpu
from jax.sharding import PartitionSpec as P

HD = 64
TXT = 226
GH = 30
GW = 45
PLEN = 256


def passed_along(value, axis, by):
    size = lax.axis_size(axis)
    pairs = [(i, i + by) for i in range(size) if 0 <= i + by < size]
    return lax.ppermute(value, axis, pairs)


def layer_norm(values, epsilon):
    centered = values - jnp.mean(values, axis=-1, keepdims=True)
    return centered * lax.rsqrt(jnp.mean(centered * centered, axis=-1, keepdims=True) + epsilon)


def rotary_tables(positions):
    video_index = jnp.maximum(positions - TXT, 0)
    is_video = positions >= TXT
    frame_index = video_index // (GH * GW)
    height_index = video_index // GW % GH
    width_index = video_index % GW
    phase_parts = []
    for coordinate, part_size in (
        (frame_index, HD // 4),
        (height_index, HD * 3 // 8),
        (width_index, HD * 3 // 8),
    ):
        frequency = 1.0 / 10000.0 ** (jnp.arange(0, part_size, 2).astype(jnp.float32) / part_size)
        phase_part = coordinate.astype(jnp.float32)[..., None] * frequency
        phase_parts.append(jnp.repeat(phase_part, 2, axis=-1))
    phase_all = jnp.concatenate(phase_parts, axis=-1)
    cosine = jnp.where(is_video[..., None], jnp.cos(phase_all), 1.0)
    sine_table = jnp.where(is_video[..., None], jnp.sin(phase_all), 0.0)
    return (cosine, sine_table)


def rotate_pairs(values, cosine, sine_table):
    paired = values.reshape(values.shape[:-1] + (values.shape[-1] // 2, 2))
    turned = jnp.stack([-paired[..., 1], paired[..., 0]], axis=-1).reshape(values.shape)
    return values * cosine + turned * sine_table


def heads_from(mixed_rows, positions, gain_pair):
    cosine, sine_table = rotary_tables(positions)
    cosine = cosine[..., None, :]
    sine_table = sine_table[..., None, :]
    keys_new = rotate_pairs(
        layer_norm(mixed_rows[..., 1, :], 1e-06) * gain_pair[1], cosine, sine_table
    ).astype(jnp.bfloat16)
    values_new = mixed_rows[..., 2, :].astype(jnp.bfloat16)
    queries = rotate_pairs(
        layer_norm(mixed_rows[..., 0, :], 1e-06) * gain_pair[0], cosine, sine_table
    ).astype(jnp.bfloat16)
    return jnp.concatenate([queries, keys_new, values_new], axis=-1)


def modulate(row_values, positions, modulation):
    is_text = (positions < TXT)[..., None]
    shifts = jnp.where(is_text, modulation[3], modulation[0])
    scales = jnp.where(is_text, modulation[4], modulation[1])
    normed = layer_norm(row_values.astype(jnp.float32), 1e-05)
    return (normed * (1.0 + scales) + shifts).astype(jnp.bfloat16)


def local(
    hidden,
    patch_counts,
    timestep,
    time_table,
    ada_weight,
    qkv_weight,
    out_weight,
    qk_gain,
    stale_kv,
    stale_inputs,
    recompute_slots,
):
    col_count = lax.axis_size("col")
    section_count = lax.axis_size("section")
    section_index = lax.axis_index("section")
    row_index = lax.axis_index("row")
    col_index = lax.axis_index("col")
    num_patches, dev_rows, num_requests, model_width = hidden.shape
    seq_length = PLEN * num_patches
    group_rows = dev_rows * col_count
    starts = jnp.cumsum(patch_counts, axis=1) - patch_counts
    slot_index = jnp.arange(seq_length, dtype=jnp.int32)
    slot_patch = slot_index // PLEN
    slot_offset = slot_index % PLEN
    positions = starts[:, slot_patch] + slot_offset[None, :]
    live_mask = slot_offset[None, :] < patch_counts[:, slot_patch]
    embedding = jax.nn.silu(time_table[timestep[0]]).astype(jnp.bfloat16)
    mod_part = jnp.dot(embedding, ada_weight[0], preferred_element_type=jnp.float32)
    modulation = lax.all_gather(mod_part, ("row", "col"), axis=0, tiled=True).reshape(
        6, model_width
    )
    weights_qkv = qkv_weight[0]
    weights_out = out_weight[0]
    gain_pair = qk_gain[0]
    scale_factor = HD ** (-0.5)

    def project(normed_part, position_table):
        piece_rows = lax.all_gather(normed_part, "col", axis=0, tiled=True)
        mixed_rows = jnp.dot(
            piece_rows.reshape(-1, model_width), weights_qkv, preferred_element_type=jnp.float32
        )
        mixed_rows = mixed_rows.reshape(piece_rows.shape[0], piece_rows.shape[1], -1, 3, HD)
        return heads_from(mixed_rows, position_table, gain_pair)

    def spread_rows(key_value):
        return lax.all_gather(key_value, "row", axis=0, tiled=True)

    rec_dev = stale_inputs.shape[1]
    rec_group = rec_dev * col_count
    rec_positions = jnp.take_along_axis(positions, recompute_slots, axis=1).T
    local_rec = lax.dynamic_slice_in_dim(
        rec_positions, (row_index * col_count + col_index) * rec_dev, rec_dev, 0
    )
    group_rec = lax.dynamic_slice_in_dim(rec_positions, row_index * rec_group, rec_group, 0)
    rec_normed = modulate(stale_inputs[0], local_rec, modulation)
    rec_heads = project(rec_normed, group_rec)
    rec_pairs = spread_rows(rec_heads[..., HD:])
    base_cache = stale_kv[0]
    for request in range(num_requests):
        base_cache = base_cache.at[recompute_slots[request], request].set(rec_pairs[:, request])
    batches = num_requests * num_patches // num_requests
    turn_count = batches + section_count - 1
    local_offsets = (
        row_index * group_rows + col_index * dev_rows + jnp.arange(dev_rows, dtype=jnp.int32)
    )
    group_offsets = row_index * group_rows + jnp.arange(group_rows, dtype=jnp.int32)

    def relay_turn(turn_index, loop_state):
        cache_table, outputs, incoming = loop_state
        batch_index = turn_index - section_index
        is_valid = (batch_index >= 0) & (batch_index < batches)
        clipped = jnp.clip(batch_index, 0, batches - 1)
        first_request = clipped // num_patches * num_requests
        patch_index = clipped % num_patches
        request_starts = starts[:, patch_index]
        local_positions = local_offsets[:, None] + request_starts[None, :]
        group_positions = group_offsets[:, None] + request_starts[None, :]
        entering = hidden[patch_index]
        inputs = jnp.where(section_index == 0, entering, incoming)
        normed = modulate(inputs, local_positions, modulation)
        heads_all = project(normed, group_positions)
        fresh_pairs = spread_rows(heads_all[..., HD:])
        block_start = (patch_index * PLEN, first_request, 0, 0)
        old_block = lax.dynamic_slice(cache_table, block_start, fresh_pairs.shape)
        new_block = jnp.where(is_valid, fresh_pairs, old_block)
        cache_table = lax.dynamic_update_slice(cache_table, new_block, block_start)
        queries = heads_all[..., :HD]
        scores = (
            jnp.einsum(
                "qrhd,krhd->rhqk",
                queries,
                cache_table[..., :HD],
                preferred_element_type=jnp.float32,
            )
            * scale_factor
        )
        weights = jnp.where(live_mask[:, None, None, :], jnp.exp(scores), 0.0)
        totals = jnp.sum(weights, axis=-1)
        attended = jnp.einsum(
            "rhqk,krhd->qrhd",
            weights.astype(jnp.bfloat16),
            cache_table[..., HD:],
            preferred_element_type=jnp.float32,
        )
        attended = (attended / jnp.transpose(totals, (2, 0, 1))[..., None]).astype(jnp.bfloat16)
        flat_rows = attended.reshape(group_rows * num_requests, -1)
        projected = (
            lax.psum_scatter(
                jnp.dot(flat_rows, weights_out, preferred_element_type=jnp.float32).astype(
                    jnp.bfloat16
                ),
                "col",
                scatter_dimension=0,
                tiled=True,
            )
            .astype(jnp.float32)
            .reshape(dev_rows, num_requests, model_width)
        )
        is_text = (local_positions < TXT)[..., None]
        gate_rows = jnp.where(is_text, modulation[5], modulation[2])
        leaving = (inputs.astype(jnp.float32) + gate_rows * projected).astype(jnp.bfloat16)
        out_start = (patch_index, 0, first_request, 0)
        current_out = lax.dynamic_slice(
            outputs, out_start, (1, dev_rows, num_requests, model_width)
        )
        written = jnp.where(is_valid, leaving[None], current_out)
        outputs = lax.dynamic_update_slice(outputs, written, out_start)
        incoming = passed_along(leaving, "section", 1)
        return (cache_table, outputs, incoming)

    outputs_start = jnp.zeros((num_patches, dev_rows, num_requests, model_width), jnp.bfloat16)
    incoming_start = jnp.zeros((dev_rows, num_requests, model_width), jnp.bfloat16)
    final_state = lax.fori_loop(
        0, turn_count, relay_turn, (base_cache, outputs_start, incoming_start)
    )
    return final_state[1][None]


HEAD_PAIR = 6 * HD
DEAD = -1e30


def block_body(patch_ref, cell_ref, x_ref, w_ref, gain_ref, cos_ref, sin_ref, bias_ref, old_ref,
               kv_ref, out_ref):
    cols, rows, reqs, toks, width = x_ref.shape
    total_rows = cols * rows * reqs * toks
    patch = patch_ref[0]
    x = x_ref[...].reshape(total_rows, width)
    mixed = jnp.dot(x, w_ref[0], preferred_element_type=jnp.float32)
    lane = lax.broadcasted_iota(jnp.int32, (total_rows, 2 * HD), 1)
    low = lane < HD
    even = lane % 2 == 0
    cosine = cos_ref[0]
    sine = sin_ref[0]

    def halves_mean(value):
        low_sum = jnp.sum(jnp.where(low, value, 0.0), axis=-1, keepdims=True)
        high_sum = jnp.sum(jnp.where(low, 0.0, value), axis=-1, keepdims=True)
        return jnp.where(low, low_sum, high_sum) * (1.0 / HD)

    def turned(value, gain):
        centered = value - halves_mean(value)
        scaled = centered * lax.rsqrt(halves_mean(centered * centered) + 1e-06) * gain
        swapped = jnp.where(even, pltpu.roll(scaled, 2 * HD - 1, 1), pltpu.roll(scaled, 1, 1))
        return scaled * cosine + swapped * sine

    raw = [mixed[:, i * 2 * HD:(i + 1) * 2 * HD] for i in range(3)]
    done = [turned(raw[i], gain_ref[i:i + 1, :]) for i in range(3)]
    first_kv = jnp.where(low, pltpu.roll(done[0], HD, 1), pltpu.roll(raw[1], HD, 1))
    second_kv = jnp.where(low, done[2], raw[2])
    first_q = jnp.where(low, done[0] * HD ** (-0.5), 0.0)
    second_q = jnp.where(low, pltpu.roll(done[1], HD, 1) * HD ** (-0.5), 0.0)
    pairs = [first_kv.astype(jnp.bfloat16), second_kv.astype(jnp.bfloat16)]
    queries = [first_q.astype(jnp.bfloat16), second_q.astype(jnp.bfloat16)]

    kv_ref[...] = old_ref[...]

    def block_of(c, w, r):
        start = ((c * rows + w) * reqs + r) * toks
        return slice(start, start + toks)

    def plen_of(c, w):
        start = (w * cols + c) * toks
        return slice(start, start + toks)

    for head in range(2):
        for c in range(cols):
            for w in range(rows):
                for r in range(reqs):
                    kv_ref[r, head, patch, plen_of(c, w), :] = pairs[head][block_of(c, w, r), :]
    plen = rows * cols * toks
    low_out = lax.broadcasted_iota(jnp.int32, (plen, 2 * HD), 1) < HD
    for r in range(reqs):
        attended = []
        for head in range(2):
            query = jnp.concatenate(
                [queries[head][block_of(c, w, r), :] for w in range(rows) for c in range(cols)],
                axis=0,
            )
            table = kv_ref[r, head].reshape(-1, 2 * HD)
            scores = lax.dot_general(
                query, table, (((1,), (1,)), ((), ())), preferred_element_type=jnp.float32
            )
            weights = jnp.exp(scores + bias_ref[r:r + 1, :])
            totals = jnp.sum(weights, axis=-1, keepdims=True)
            summed = jnp.dot(
                weights.astype(jnp.bfloat16), table, preferred_element_type=jnp.float32
            )
            attended.append(summed / totals)
        both = jnp.where(low_out, pltpu.roll(attended[0], HD, 1), attended[1])
        both = both.astype(jnp.bfloat16)
        for w in range(rows):
            for c in range(cols):
                out_ref[w, c, r] = both[plen_of(c, w), :]


def block_call(patch, cell, x, weights, gains, cosine, sine, bias, cache):
    cols, rows, reqs, toks, width = x.shape
    pair_count = cache.shape[1] // 2
    patches, plen = cache.shape[2], cache.shape[3]
    total_rows = cols * rows * reqs * toks
    flops = 2 * total_rows * width * HEAD_PAIR * pair_count
    flops += 8 * total_rows * patches * plen * HD * pair_count * 2
    grid_spec = pltpu.PrefetchScalarGridSpec(
        num_scalar_prefetch=2,
        grid=(pair_count,),
        in_specs=[
            pl.BlockSpec(x.shape, lambda j, p, m: (0, 0, 0, 0, 0)),
            pl.BlockSpec((1, width, HEAD_PAIR), lambda j, p, m: (0, 0, m[0] * pair_count + j)),
            pl.BlockSpec(gains.shape, lambda j, p, m: (0, 0)),
            pl.BlockSpec((1, total_rows, 2 * HD), lambda j, p, m: (p[0], 0, 0)),
            pl.BlockSpec((1, total_rows, 2 * HD), lambda j, p, m: (p[0], 0, 0)),
            pl.BlockSpec(bias.shape, lambda j, p, m: (0, 0)),
            pl.BlockSpec((reqs, 2, patches, plen, 2 * HD), lambda j, p, m: (0, j, 0, 0, 0)),
        ],
        out_specs=[
            pl.BlockSpec((reqs, 2, patches, plen, 2 * HD), lambda j, p, m: (0, j, 0, 0, 0)),
            pl.BlockSpec((rows, cols, reqs, toks, 2 * HD), lambda j, p, m: (0, 0, 0, 0, j)),
        ],
    )
    return pl.pallas_call(
        block_body,
        grid_spec=grid_spec,
        out_shape=[
            jax.ShapeDtypeStruct(cache.shape, jnp.bfloat16),
            jax.ShapeDtypeStruct((rows, cols, reqs, toks, pair_count * 2 * HD), jnp.bfloat16),
        ],
        compiler_params=pltpu.CompilerParams(vmem_limit_bytes=44 * 1024 * 1024),
        cost_estimate=pl.CostEstimate(
            flops=flops, bytes_accessed=20 * 1024 * 1024,
            transcendentals=2 * pair_count * total_rows * patches * plen,
        ),
    )(patch, cell, x, weights, gains, cosine, sine, bias, cache)


def modulate_split(values, positions, modulation):
    is_text = (positions < TXT)[..., None]
    shifts = jnp.where(is_text, modulation[3], modulation[0])
    scales = jnp.where(is_text, modulation[4], modulation[1])
    normed = layer_norm(values.astype(jnp.float32), 1e-05)
    return (normed * (1.0 + scales) + shifts).astype(jnp.bfloat16)


def gather_cells(value):
    return lax.all_gather(lax.all_gather(value, "row", axis=0), "col", axis=0)


def local_split(
    hidden,
    patch_counts,
    timestep,
    time_table,
    ada_weight,
    qkv_weight,
    out_weight,
    qk_gain,
    stale_kv,
    stale_inputs,
    recompute_slots,
):
    cols = lax.axis_size("col")
    rows = lax.axis_size("row")
    section_count = lax.axis_size("section")
    section = lax.axis_index("section")
    row = lax.axis_index("row")
    col = lax.axis_index("col")
    num_patches, toks, reqs, width = hidden.shape
    seq = PLEN * num_patches
    heads_here = stale_kv.shape[3] // rows
    starts = jnp.cumsum(patch_counts, axis=1) - patch_counts
    slots = jnp.arange(seq, dtype=jnp.int32)
    positions = starts[:, slots // PLEN] + slots[None, :] % PLEN
    live = slots[None, :] % PLEN < patch_counts[:, slots // PLEN]
    bias = jnp.where(live, 0.0, DEAD).astype(jnp.float32)

    embedding = jax.nn.silu(time_table[timestep[0]]).astype(jnp.bfloat16)
    mod_part = jnp.dot(embedding, ada_weight[0], preferred_element_type=jnp.float32)
    modulation = lax.all_gather(mod_part, ("row", "col"), axis=0, tiled=True).reshape(6, width)

    cell_positions = positions.reshape(reqs, num_patches, rows, cols, toks)
    cell_positions = cell_positions.transpose(1, 3, 2, 0, 4).reshape(num_patches, -1)
    cosine, sine = rotary_tables(cell_positions)
    signs = jnp.where(jnp.arange(HD) % 2 == 0, -1.0, 1.0)
    sine = sine * signs
    cosine = jnp.concatenate([cosine, cosine], axis=-1)
    sine = jnp.concatenate([sine, sine], axis=-1)
    gain_q, gain_k = qk_gain[0, 0], qk_gain[0, 1]
    ones = jnp.ones_like(gain_q)
    gains = jnp.stack([
        jnp.concatenate([gain_q, gain_k]),
        jnp.concatenate([ones, gain_q]),
        jnp.concatenate([gain_k, ones]),
    ])

    rec = recompute_slots.shape[1]
    rec_toks = rec // (rows * cols)
    rec_positions = jnp.take_along_axis(positions, recompute_slots, axis=1)
    my_rec = lax.dynamic_slice_in_dim(rec_positions, (row * cols + col) * rec_toks, rec_toks, 1)
    rec_normed = modulate_split(stale_inputs[0], my_rec.T, modulation)
    rec_all = gather_cells(rec_normed)

    def by_cell(table):
        table = table.reshape(reqs, rows, cols, rec_toks).transpose(2, 1, 3, 0)
        return table.reshape(-1, reqs)

    rec_places = by_cell(rec_positions)
    rec_slots = by_cell(recompute_slots)
    per_row = heads_here * 3 * HD
    weights_here = lax.dynamic_slice_in_dim(qkv_weight[0], row * per_row, per_row, 1)
    rec_mixed = jnp.dot(
        rec_all.reshape(-1, width), weights_here, preferred_element_type=jnp.float32
    ).reshape(rec, reqs, heads_here, 3, HD)
    rec_pairs = heads_from(rec_mixed, rec_places, qk_gain[0])[..., HD:]
    stale_here = lax.dynamic_slice_in_dim(stale_kv[0], row * heads_here, heads_here, 2)
    stale_here = stale_here.transpose(1, 2, 0, 3)
    match = (slots[None, :, None] == rec_slots.T[:, None, :])
    placed = jnp.einsum(
        "rsi,irhd->rhsd", match.astype(jnp.bfloat16), rec_pairs,
        preferred_element_type=jnp.float32,
    ).astype(jnp.bfloat16)
    replaced = jnp.any(match, axis=-1)[:, None, :, None]
    cache = jnp.where(replaced, placed, stale_here)
    cache = cache.reshape(reqs, heads_here, num_patches, PLEN, 2 * HD)

    entering = hidden.transpose(0, 2, 1, 3)
    out_rows = out_weight[0].reshape(rows, heads_here * HD, width)
    my_offsets = (row * cols + col) * toks + jnp.arange(toks, dtype=jnp.int32)
    cell = jnp.reshape(row, (1,)).astype(jnp.int32)
    leavings = []
    incoming = entering[0]
    for turn in range(num_patches + section_count - 1):
        patch = jnp.clip(turn - section, 0, num_patches - 1).astype(jnp.int32)
        my_positions = starts[:, patch][:, None] + my_offsets[None, :]
        if turn == 0 or turn >= num_patches:
            inputs = incoming
        else:
            inputs = jnp.where(section == 0, entering[turn], incoming)
        normed = modulate_split(inputs, my_positions, modulation)
        cache, attended = block_call(
            patch.reshape(1), cell, gather_cells(normed), qkv_weight, gains, cosine, sine, bias,
            cache,
        )
        returned = lax.all_to_all(attended, "row", 0, 0, tiled=True)
        returned = returned.transpose(1, 2, 3, 0, 4).reshape(cols * reqs * toks, -1)
        partial = jnp.dot(
            returned, out_weight[0], preferred_element_type=jnp.float32
        ).astype(jnp.bfloat16).reshape(cols, reqs, toks, width)
        mine = lax.dynamic_index_in_dim(partial, col, 0, False)
        other = lax.dynamic_index_in_dim(partial, 1 - col, 0, False)
        other = lax.ppermute(other, "col", [(0, 1), (1, 0)])
        projected = mine.astype(jnp.float32) + other.astype(jnp.float32)
        is_text = (my_positions < TXT)[..., None]
        gate_rows = jnp.where(is_text, modulation[5], modulation[2])
        leaving = (inputs.astype(jnp.float32) + gate_rows * projected).astype(jnp.bfloat16)
        leavings.append(leaving)
        if turn < num_patches + section_count - 2:
            incoming = passed_along(leaving, "section", 1)
    stacked = jnp.stack(leavings)
    mine = lax.dynamic_slice_in_dim(stacked, section, num_patches, 0)
    return mine.transpose(0, 2, 1, 3)[None]


def fits_split(mesh):
    heads = 48 // mesh.shape["col"]
    return mesh.shape["col"] == 2 and heads % (2 * mesh.shape["row"]) == 0


def solution(mesh):
    return jax.shard_map(
        local_split if fits_split(mesh) else local,
        mesh=mesh,
        in_specs=(
            P(None, ("row", "col"), None, None),
            P(),
            P(),
            P(),
            P("section", None, ("row", "col")),
            P("section", None, "col"),
            P("section", "col", None),
            P("section", None, None),
            P("section", None, None, "col", None),
            P("section", ("row", "col"), None, None),
            P(),
        ),
        out_specs=P("section", None, ("row", "col"), None, None),
        check_vma=False,
    )
```

```python
import jax
import jax.numpy as jnp
from jax import lax
from jax.experimental import pallas as pl
from jax.experimental.pallas import tpu as pltpu
from jax.sharding import PartitionSpec as P

HD = 64
TXT = 226
GH = 30
GW = 45
PLEN = 256


def passed_along(value, axis, by):
    size = lax.axis_size(axis)
    pairs = [(i, i + by) for i in range(size) if 0 <= i + by < size]
    return lax.ppermute(value, axis, pairs)


def layer_norm(values, epsilon):
    centered = values - jnp.mean(values, axis=-1, keepdims=True)
    return centered * lax.rsqrt(jnp.mean(centered * centered, axis=-1, keepdims=True) + epsilon)


def rotary_tables(positions):
    video_index = jnp.maximum(positions - TXT, 0)
    is_video = positions >= TXT
    frame_index = video_index // (GH * GW)
    height_index = video_index // GW % GH
    width_index = video_index % GW
    phase_parts = []
    for coordinate, part_size in (
        (frame_index, HD // 4),
        (height_index, HD * 3 // 8),
        (width_index, HD * 3 // 8),
    ):
        frequency = 1.0 / 10000.0 ** (jnp.arange(0, part_size, 2).astype(jnp.float32) / part_size)
        phase_part = coordinate.astype(jnp.float32)[..., None] * frequency
        phase_parts.append(jnp.repeat(phase_part, 2, axis=-1))
    phase_all = jnp.concatenate(phase_parts, axis=-1)
    cosine = jnp.where(is_video[..., None], jnp.cos(phase_all), 1.0)
    sine_table = jnp.where(is_video[..., None], jnp.sin(phase_all), 0.0)
    return (cosine, sine_table)


def rotate_pairs(values, cosine, sine_table):
    paired = values.reshape(values.shape[:-1] + (values.shape[-1] // 2, 2))
    turned = jnp.stack([-paired[..., 1], paired[..., 0]], axis=-1).reshape(values.shape)
    return values * cosine + turned * sine_table


def heads_from(mixed_rows, positions, gain_pair):
    cosine, sine_table = rotary_tables(positions)
    cosine = cosine[..., None, :]
    sine_table = sine_table[..., None, :]
    keys_new = rotate_pairs(
        layer_norm(mixed_rows[..., 1, :], 1e-06) * gain_pair[1], cosine, sine_table
    ).astype(jnp.bfloat16)
    values_new = mixed_rows[..., 2, :].astype(jnp.bfloat16)
    queries = rotate_pairs(
        layer_norm(mixed_rows[..., 0, :], 1e-06) * gain_pair[0], cosine, sine_table
    ).astype(jnp.bfloat16)
    return jnp.concatenate([queries, keys_new, values_new], axis=-1)


def modulate(row_values, positions, modulation):
    is_text = (positions < TXT)[..., None]
    shifts = jnp.where(is_text, modulation[3], modulation[0])
    scales = jnp.where(is_text, modulation[4], modulation[1])
    normed = layer_norm(row_values.astype(jnp.float32), 1e-05)
    return (normed * (1.0 + scales) + shifts).astype(jnp.bfloat16)


def local(
    hidden,
    patch_counts,
    timestep,
    time_table,
    ada_weight,
    qkv_weight,
    out_weight,
    qk_gain,
    stale_kv,
    stale_inputs,
    recompute_slots,
):
    col_count = lax.axis_size("col")
    section_count = lax.axis_size("section")
    section_index = lax.axis_index("section")
    row_index = lax.axis_index("row")
    col_index = lax.axis_index("col")
    num_patches, dev_rows, num_requests, model_width = hidden.shape
    seq_length = PLEN * num_patches
    group_rows = dev_rows * col_count
    starts = jnp.cumsum(patch_counts, axis=1) - patch_counts
    slot_index = jnp.arange(seq_length, dtype=jnp.int32)
    slot_patch = slot_index // PLEN
    slot_offset = slot_index % PLEN
    positions = starts[:, slot_patch] + slot_offset[None, :]
    live_mask = slot_offset[None, :] < patch_counts[:, slot_patch]
    embedding = jax.nn.silu(time_table[timestep[0]]).astype(jnp.bfloat16)
    mod_part = jnp.dot(embedding, ada_weight[0], preferred_element_type=jnp.float32)
    modulation = lax.all_gather(mod_part, ("row", "col"), axis=0, tiled=True).reshape(
        6, model_width
    )
    weights_qkv = qkv_weight[0]
    weights_out = out_weight[0]
    gain_pair = qk_gain[0]
    scale_factor = HD ** (-0.5)

    def project(normed_part, position_table):
        piece_rows = lax.all_gather(normed_part, "col", axis=0, tiled=True)
        mixed_rows = jnp.dot(
            piece_rows.reshape(-1, model_width), weights_qkv, preferred_element_type=jnp.float32
        )
        mixed_rows = mixed_rows.reshape(piece_rows.shape[0], piece_rows.shape[1], -1, 3, HD)
        return heads_from(mixed_rows, position_table, gain_pair)

    def spread_rows(key_value):
        return lax.all_gather(key_value, "row", axis=0, tiled=True)

    rec_dev = stale_inputs.shape[1]
    rec_group = rec_dev * col_count
    rec_positions = jnp.take_along_axis(positions, recompute_slots, axis=1).T
    local_rec = lax.dynamic_slice_in_dim(
        rec_positions, (row_index * col_count + col_index) * rec_dev, rec_dev, 0
    )
    group_rec = lax.dynamic_slice_in_dim(rec_positions, row_index * rec_group, rec_group, 0)
    rec_normed = modulate(stale_inputs[0], local_rec, modulation)
    rec_heads = project(rec_normed, group_rec)
    rec_pairs = spread_rows(rec_heads[..., HD:])
    base_cache = stale_kv[0]
    for request in range(num_requests):
        base_cache = base_cache.at[recompute_slots[request], request].set(rec_pairs[:, request])
    batches = num_requests * num_patches // num_requests
    turn_count = batches + section_count - 1
    local_offsets = (
        row_index * group_rows + col_index * dev_rows + jnp.arange(dev_rows, dtype=jnp.int32)
    )
    group_offsets = row_index * group_rows + jnp.arange(group_rows, dtype=jnp.int32)

    def relay_turn(turn_index, loop_state):
        cache_table, outputs, incoming = loop_state
        batch_index = turn_index - section_index
        is_valid = (batch_index >= 0) & (batch_index < batches)
        clipped = jnp.clip(batch_index, 0, batches - 1)
        first_request = clipped // num_patches * num_requests
        patch_index = clipped % num_patches
        request_starts = starts[:, patch_index]
        local_positions = local_offsets[:, None] + request_starts[None, :]
        group_positions = group_offsets[:, None] + request_starts[None, :]
        entering = hidden[patch_index]
        inputs = jnp.where(section_index == 0, entering, incoming)
        normed = modulate(inputs, local_positions, modulation)
        heads_all = project(normed, group_positions)
        fresh_pairs = spread_rows(heads_all[..., HD:])
        block_start = (patch_index * PLEN, first_request, 0, 0)
        old_block = lax.dynamic_slice(cache_table, block_start, fresh_pairs.shape)
        new_block = jnp.where(is_valid, fresh_pairs, old_block)
        cache_table = lax.dynamic_update_slice(cache_table, new_block, block_start)
        queries = heads_all[..., :HD]
        scores = (
            jnp.einsum(
                "qrhd,krhd->rhqk",
                queries,
                cache_table[..., :HD],
                preferred_element_type=jnp.float32,
            )
            * scale_factor
        )
        weights = jnp.where(live_mask[:, None, None, :], jnp.exp(scores), 0.0)
        totals = jnp.sum(weights, axis=-1)
        attended = jnp.einsum(
            "rhqk,krhd->qrhd",
            weights.astype(jnp.bfloat16),
            cache_table[..., HD:],
            preferred_element_type=jnp.float32,
        )
        attended = (attended / jnp.transpose(totals, (2, 0, 1))[..., None]).astype(jnp.bfloat16)
        flat_rows = attended.reshape(group_rows * num_requests, -1)
        projected = (
            lax.psum_scatter(
                jnp.dot(flat_rows, weights_out, preferred_element_type=jnp.float32).astype(
                    jnp.bfloat16
                ),
                "col",
                scatter_dimension=0,
                tiled=True,
            )
            .astype(jnp.float32)
            .reshape(dev_rows, num_requests, model_width)
        )
        is_text = (local_positions < TXT)[..., None]
        gate_rows = jnp.where(is_text, modulation[5], modulation[2])
        leaving = (inputs.astype(jnp.float32) + gate_rows * projected).astype(jnp.bfloat16)
        out_start = (patch_index, 0, first_request, 0)
        current_out = lax.dynamic_slice(
            outputs, out_start, (1, dev_rows, num_requests, model_width)
        )
        written = jnp.where(is_valid, leaving[None], current_out)
        outputs = lax.dynamic_update_slice(outputs, written, out_start)
        incoming = passed_along(leaving, "section", 1)
        return (cache_table, outputs, incoming)

    outputs_start = jnp.zeros((num_patches, dev_rows, num_requests, model_width), jnp.bfloat16)
    incoming_start = jnp.zeros((dev_rows, num_requests, model_width), jnp.bfloat16)
    final_state = lax.fori_loop(
        0, turn_count, relay_turn, (base_cache, outputs_start, incoming_start)
    )
    return final_state[1][None]


HEAD_PAIR = 6 * HD
DEAD = -1e30


def block_body(patch_ref, cell_ref, x_ref, w_ref, gain_ref, cos_ref, sin_ref, bias_ref, old_ref,
               kv_ref, out_ref):
    cols, rows, reqs, toks, width = x_ref.shape
    total_rows = cols * rows * reqs * toks
    patch = patch_ref[0]
    x = x_ref[...].reshape(total_rows, width)
    mixed = jnp.dot(x, w_ref[0], preferred_element_type=jnp.float32)
    lane = lax.broadcasted_iota(jnp.int32, (total_rows, 2 * HD), 1)
    low = lane < HD
    even = lane % 2 == 0
    cosine = cos_ref[0]
    sine = sin_ref[0]

    def halves_mean(value):
        low_sum = jnp.sum(jnp.where(low, value, 0.0), axis=-1, keepdims=True)
        high_sum = jnp.sum(jnp.where(low, 0.0, value), axis=-1, keepdims=True)
        return jnp.where(low, low_sum, high_sum) * (1.0 / HD)

    def turned(value, gain):
        centered = value - halves_mean(value)
        scaled = centered * lax.rsqrt(halves_mean(centered * centered) + 1e-06) * gain
        swapped = jnp.where(even, pltpu.roll(scaled, 2 * HD - 1, 1), pltpu.roll(scaled, 1, 1))
        return scaled * cosine + swapped * sine

    raw = [mixed[:, i * 2 * HD:(i + 1) * 2 * HD] for i in range(3)]
    done = [turned(raw[i], gain_ref[i:i + 1, :]) for i in range(3)]
    first_kv = jnp.where(low, pltpu.roll(done[0], HD, 1), pltpu.roll(raw[1], HD, 1))
    second_kv = jnp.where(low, done[2], raw[2])
    first_q = jnp.where(low, done[0] * HD ** (-0.5), 0.0)
    second_q = jnp.where(low, pltpu.roll(done[1], HD, 1) * HD ** (-0.5), 0.0)
    pairs = [first_kv.astype(jnp.bfloat16), second_kv.astype(jnp.bfloat16)]
    queries = [first_q.astype(jnp.bfloat16), second_q.astype(jnp.bfloat16)]

    kv_ref[...] = old_ref[...]

    def block_of(c, w, r):
        start = ((c * rows + w) * reqs + r) * toks
        return slice(start, start + toks)

    def plen_of(c, w):
        start = (w * cols + c) * toks
        return slice(start, start + toks)

    for head in range(2):
        for c in range(cols):
            for w in range(rows):
                for r in range(reqs):
                    kv_ref[r, head, patch, plen_of(c, w), :] = pairs[head][block_of(c, w, r), :]
    plen = rows * cols * toks
    low_out = lax.broadcasted_iota(jnp.int32, (plen, 2 * HD), 1) < HD
    for r in range(reqs):
        attended = []
        for head in range(2):
            query = jnp.concatenate(
                [queries[head][block_of(c, w, r), :] for w in range(rows) for c in range(cols)],
                axis=0,
            )
            table = kv_ref[r, head].reshape(-1, 2 * HD)
            scores = lax.dot_general(
                query, table, (((1,), (1,)), ((), ())), preferred_element_type=jnp.float32
            )
            weights = jnp.exp(scores + bias_ref[r:r + 1, :])
            totals = jnp.sum(weights, axis=-1, keepdims=True)
            summed = jnp.dot(
                weights.astype(jnp.bfloat16), table, preferred_element_type=jnp.float32
            )
            attended.append(summed / totals)
        both = jnp.where(low_out, pltpu.roll(attended[0], HD, 1), attended[1])
        both = both.astype(jnp.bfloat16)
        for w in range(rows):
            for c in range(cols):
                out_ref[w, c, r] = both[plen_of(c, w), :]


def block_call(patch, cell, x, weights, gains, cosine, sine, bias, cache):
    cols, rows, reqs, toks, width = x.shape
    pair_count = cache.shape[1] // 2
    patches, plen = cache.shape[2], cache.shape[3]
    total_rows = cols * rows * reqs * toks
    flops = 2 * total_rows * width * HEAD_PAIR * pair_count
    flops += 8 * total_rows * patches * plen * HD * pair_count * 2
    grid_spec = pltpu.PrefetchScalarGridSpec(
        num_scalar_prefetch=2,
        grid=(pair_count,),
        in_specs=[
            pl.BlockSpec(x.shape, lambda j, p, m: (0, 0, 0, 0, 0)),
            pl.BlockSpec((1, width, HEAD_PAIR), lambda j, p, m: (0, 0, m[0] * pair_count + j)),
            pl.BlockSpec(gains.shape, lambda j, p, m: (0, 0)),
            pl.BlockSpec((1, total_rows, 2 * HD), lambda j, p, m: (p[0], 0, 0)),
            pl.BlockSpec((1, total_rows, 2 * HD), lambda j, p, m: (p[0], 0, 0)),
            pl.BlockSpec(bias.shape, lambda j, p, m: (0, 0)),
            pl.BlockSpec((reqs, 2, patches, plen, 2 * HD), lambda j, p, m: (0, j, 0, 0, 0)),
        ],
        out_specs=[
            pl.BlockSpec((reqs, 2, patches, plen, 2 * HD), lambda j, p, m: (0, j, 0, 0, 0)),
            pl.BlockSpec((rows, cols, reqs, toks, 2 * HD), lambda j, p, m: (0, 0, 0, 0, j)),
        ],
    )
    return pl.pallas_call(
        block_body,
        grid_spec=grid_spec,
        out_shape=[
            jax.ShapeDtypeStruct(cache.shape, jnp.bfloat16),
            jax.ShapeDtypeStruct((rows, cols, reqs, toks, pair_count * 2 * HD), jnp.bfloat16),
        ],
        compiler_params=pltpu.CompilerParams(vmem_limit_bytes=44 * 1024 * 1024),
        cost_estimate=pl.CostEstimate(
            flops=flops, bytes_accessed=20 * 1024 * 1024,
            transcendentals=2 * pair_count * total_rows * patches * plen,
        ),
    )(patch, cell, x, weights, gains, cosine, sine, bias, cache)


def modulate_split(values, positions, modulation):
    is_text = (positions < TXT)[..., None]
    shifts = jnp.where(is_text, modulation[3], modulation[0])
    scales = jnp.where(is_text, modulation[4], modulation[1])
    normed = layer_norm(values.astype(jnp.float32), 1e-05)
    return (normed * (1.0 + scales) + shifts).astype(jnp.bfloat16)


def gather_body(x_ref, out_ref, own_sem, line_send, line_recv, side_send, side_recv):
    chunks = x_ref.shape[0]
    rows = out_ref.shape[1]
    w = lax.axis_index("row")
    c = lax.axis_index("col")
    sibling = {"col": 1 - c}
    barrier = pltpu.get_barrier_semaphore()
    has = {1: w < rows - 1, -1: w > 0}

    def greet(way):
        @pl.when(has[way])
        def _():
            pl.semaphore_signal(barrier, inc=1, device_id={"row": w + way},
                                device_id_type=pl.DeviceIdType.MESH)

    pl.semaphore_signal(barrier, inc=1, device_id=sibling, device_id_type=pl.DeviceIdType.MESH)
    greet(1)
    greet(-1)
    inside = has[1] & has[-1]

    @pl.when(inside)
    def _():
        pl.semaphore_wait(barrier, 3)

    @pl.when(jnp.logical_not(inside))
    def _():
        pl.semaphore_wait(barrier, 2)

    def line_copy(way, step, chunk):
        block = w - way * step
        source = x_ref.at[chunk] if step == 0 else out_ref.at[c, block, chunk]
        lane = 0 if way == 1 else 1
        return pltpu.make_async_remote_copy(
            src_ref=source, dst_ref=out_ref.at[c, block, chunk],
            send_sem=line_send.at[lane, step, chunk], recv_sem=line_recv.at[lane, step, chunk],
            device_id={"row": w + way}, device_id_type=pl.DeviceIdType.MESH,
        )

    def arrival(way, step, chunk):
        block = w - way * (step + 1)
        lane = 0 if way == 1 else 1
        return pltpu.make_async_remote_copy(
            src_ref=x_ref.at[chunk], dst_ref=out_ref.at[c, block, chunk],
            send_sem=line_send.at[lane, step, chunk], recv_sem=line_recv.at[lane, step, chunk],
            device_id={"row": w + way}, device_id_type=pl.DeviceIdType.MESH,
        )

    def side_copy(place, block, chunk):
        source = x_ref.at[chunk] if place == 0 else out_ref.at[c, block, chunk]
        return pltpu.make_async_remote_copy(
            src_ref=source, dst_ref=out_ref.at[c, block, chunk],
            send_sem=side_send.at[place, chunk], recv_sem=side_recv.at[place, chunk],
            device_id=sibling, device_id_type=pl.DeviceIdType.MESH,
        )

    def side_arrival(place, block, chunk):
        return pltpu.make_async_remote_copy(
            src_ref=x_ref.at[chunk], dst_ref=out_ref.at[1 - c, block, chunk],
            send_sem=side_send.at[place, chunk], recv_sem=side_recv.at[place, chunk],
            device_id=sibling, device_id_type=pl.DeviceIdType.MESH,
        )

    def arrives(way, step):
        return w >= step + 1 if way == 1 else w <= rows - 2 - step

    def leaves(way, step):
        held = w >= step if way == 1 else w <= rows - 1 - step
        return has[way] & held

    def place_of(way, step):
        return 1 + step if way == 1 else rows + step

    for chunk in range(chunks):
        for way in (1, -1):
            @pl.when(leaves(way, 0))
            def _():
                line_copy(way, 0, chunk).start()
    own = []
    for chunk in range(chunks):
        side_copy(0, w, chunk).start()
        kept = pltpu.make_async_copy(x_ref.at[chunk], out_ref.at[c, w, chunk], own_sem.at[chunk])
        kept.start()
        own.append(kept)
    for step in range(rows - 1):
        for chunk in range(chunks):
            for way in (1, -1):
                @pl.when(arrives(way, step))
                def _():
                    arrival(way, step, chunk).wait_recv()
                    if step + 1 < rows - 1:
                        @pl.when(leaves(way, step + 1))
                        def _():
                            line_copy(way, step + 1, chunk).start()
                    side_copy(place_of(way, step), w - way * (step + 1), chunk).start()
    for chunk in range(chunks):
        own[chunk].wait()
        side_copy(0, w, chunk).wait_send()
        side_arrival(0, w, chunk).wait_recv()
        for step in range(rows - 1):
            for way in (1, -1):
                @pl.when(leaves(way, step))
                def _():
                    line_copy(way, step, chunk).wait_send()

                @pl.when(arrives(way, step))
                def _():
                    block = w - way * (step + 1)
                    side_copy(place_of(way, step), block, chunk).wait_send()
                    side_arrival(place_of(way, step), block, chunk).wait_recv()


def gather_tokens(value, rows, cols, number):
    chunks = value.shape[0]
    steps = rows - 1
    return pl.pallas_call(
        gather_body,
        out_shape=jax.ShapeDtypeStruct((cols, rows) + value.shape, value.dtype),
        in_specs=[pl.BlockSpec(memory_space=pl.ANY)],
        out_specs=pl.BlockSpec(memory_space=pl.ANY),
        scratch_shapes=[
            pltpu.SemaphoreType.DMA((chunks,)),
            pltpu.SemaphoreType.DMA((2, steps, chunks)),
            pltpu.SemaphoreType.DMA((2, steps, chunks)),
            pltpu.SemaphoreType.DMA((2 * steps + 1, chunks)),
            pltpu.SemaphoreType.DMA((2 * steps + 1, chunks)),
        ],
        compiler_params=pltpu.CompilerParams(collective_id=number, has_side_effects=True),
        cost_estimate=pl.CostEstimate(flops=0, bytes_accessed=40 * 1024 * 1024, transcendentals=0),
    )(value)


def exchange_body(x_ref, out_ref, own_sem, send_sem, recv_sem):
    rows = x_ref.shape[0]
    w = lax.axis_index("row")
    barrier = pltpu.get_barrier_semaphore()
    for way in range(1, rows):
        pl.semaphore_signal(barrier, inc=1, device_id={"row": lax.rem(w + way, rows)},
                            device_id_type=pl.DeviceIdType.MESH)
    pl.semaphore_wait(barrier, rows - 1)
    copies = []
    for way in range(1, rows):
        target = lax.rem(w + way, rows)
        copy = pltpu.make_async_remote_copy(
            src_ref=x_ref.at[target], dst_ref=out_ref.at[w],
            send_sem=send_sem.at[way - 1], recv_sem=recv_sem.at[way - 1],
            device_id={"row": target}, device_id_type=pl.DeviceIdType.MESH,
        )
        copy.start()
        copies.append(copy)
    kept = pltpu.make_async_copy(x_ref.at[w], out_ref.at[w], own_sem)
    kept.start()
    for copy in copies:
        copy.wait()
    kept.wait()


def exchange_rows(value, number):
    rows = value.shape[0]
    return pl.pallas_call(
        exchange_body,
        out_shape=jax.ShapeDtypeStruct(value.shape, value.dtype),
        in_specs=[pl.BlockSpec(memory_space=pl.ANY)],
        out_specs=pl.BlockSpec(memory_space=pl.ANY),
        scratch_shapes=[
            pltpu.SemaphoreType.DMA,
            pltpu.SemaphoreType.DMA((rows - 1,)),
            pltpu.SemaphoreType.DMA((rows - 1,)),
        ],
        compiler_params=pltpu.CompilerParams(collective_id=number, has_side_effects=True),
        cost_estimate=pl.CostEstimate(flops=0, bytes_accessed=16 * 1024 * 1024, transcendentals=0),
    )(value)


def local_split(
    hidden,
    patch_counts,
    timestep,
    time_table,
    ada_weight,
    qkv_weight,
    out_weight,
    qk_gain,
    stale_kv,
    stale_inputs,
    recompute_slots,
):
    cols = lax.axis_size("col")
    rows = lax.axis_size("row")
    section_count = lax.axis_size("section")
    section = lax.axis_index("section")
    row = lax.axis_index("row")
    col = lax.axis_index("col")
    num_patches, toks, reqs, width = hidden.shape
    seq = PLEN * num_patches
    heads_here = stale_kv.shape[3] // rows
    starts = jnp.cumsum(patch_counts, axis=1) - patch_counts
    slots = jnp.arange(seq, dtype=jnp.int32)
    positions = starts[:, slots // PLEN] + slots[None, :] % PLEN
    live = slots[None, :] % PLEN < patch_counts[:, slots // PLEN]
    bias = jnp.where(live, 0.0, DEAD).astype(jnp.float32)

    embedding = jax.nn.silu(time_table[timestep[0]]).astype(jnp.bfloat16)
    mod_part = jnp.dot(embedding, ada_weight[0], preferred_element_type=jnp.float32)
    modulation = lax.all_gather(mod_part, ("row", "col"), axis=0, tiled=True).reshape(6, width)

    cell_positions = positions.reshape(reqs, num_patches, rows, cols, toks)
    cell_positions = cell_positions.transpose(1, 3, 2, 0, 4).reshape(num_patches, -1)
    cosine, sine = rotary_tables(cell_positions)
    signs = jnp.where(jnp.arange(HD) % 2 == 0, -1.0, 1.0)
    sine = sine * signs
    cosine = jnp.concatenate([cosine, cosine], axis=-1)
    sine = jnp.concatenate([sine, sine], axis=-1)
    gain_q, gain_k = qk_gain[0, 0], qk_gain[0, 1]
    ones = jnp.ones_like(gain_q)
    gains = jnp.stack([
        jnp.concatenate([gain_q, gain_k]),
        jnp.concatenate([ones, gain_q]),
        jnp.concatenate([gain_k, ones]),
    ])

    rec = recompute_slots.shape[1]
    rec_toks = rec // (rows * cols)
    rec_positions = jnp.take_along_axis(positions, recompute_slots, axis=1)
    my_rec = lax.dynamic_slice_in_dim(rec_positions, (row * cols + col) * rec_toks, rec_toks, 1)
    rec_normed = modulate_split(stale_inputs[0], my_rec.T, modulation)
    entering = hidden.transpose(0, 2, 1, 3)
    my_offsets = (row * cols + col) * toks + jnp.arange(toks, dtype=jnp.int32)
    rec_part = rec_normed.reshape(rec_toks * reqs, width)
    padded = -(-rec_toks * reqs // toks) * toks
    rec_part = jnp.pad(rec_part, ((0, padded - rec_toks * reqs), (0, 0)))
    first_positions = starts[:, 0][:, None] + my_offsets[None, :]
    first_normed = modulate_split(entering[0], first_positions, modulation)
    first_all = gather_tokens(
        jnp.concatenate([first_normed, rec_part.reshape(-1, toks, width)], axis=0), rows, cols, 0
    )
    rec_all = first_all[:, :, reqs:].reshape(cols, rows, padded, width)
    rec_all = rec_all[:, :, :rec_toks * reqs]

    def by_cell(table):
        table = table.reshape(reqs, rows, cols, rec_toks).transpose(2, 1, 3, 0)
        return table.reshape(-1, reqs)

    rec_places = by_cell(rec_positions)
    rec_slots = by_cell(recompute_slots)
    per_row = heads_here * 3 * HD
    weights_here = lax.dynamic_slice_in_dim(qkv_weight[0], row * per_row, per_row, 1)
    rec_mixed = jnp.dot(
        rec_all.reshape(-1, width), weights_here, preferred_element_type=jnp.float32
    ).reshape(rec, reqs, heads_here, 3, HD)
    rec_pairs = heads_from(rec_mixed, rec_places, qk_gain[0])[..., HD:]
    stale_here = lax.dynamic_slice_in_dim(stale_kv[0], row * heads_here, heads_here, 2)
    stale_here = stale_here.transpose(1, 2, 0, 3)
    match = (slots[None, :, None] == rec_slots.T[:, None, :])
    placed = jnp.einsum(
        "rsi,irhd->rhsd", match.astype(jnp.bfloat16), rec_pairs,
        preferred_element_type=jnp.float32,
    ).astype(jnp.bfloat16)
    replaced = jnp.any(match, axis=-1)[:, None, :, None]
    cache = jnp.where(replaced, placed, stale_here)
    cache = cache.reshape(reqs, heads_here, num_patches, PLEN, 2 * HD)

    cell = jnp.reshape(row, (1,)).astype(jnp.int32)
    leavings = []
    incoming = entering[0]
    for turn in range(num_patches + section_count - 1):
        patch = jnp.clip(turn - section, 0, num_patches - 1).astype(jnp.int32)
        my_positions = starts[:, patch][:, None] + my_offsets[None, :]
        if turn == 0 or turn >= num_patches:
            inputs = incoming
        else:
            inputs = jnp.where(section == 0, entering[turn], incoming)
        if turn == 0:
            tokens = first_all[:, :, :reqs]
        else:
            normed = modulate_split(inputs, my_positions, modulation)
            tokens = gather_tokens(normed, rows, cols, 1)
        cache, attended = block_call(
            patch.reshape(1), cell, tokens, qkv_weight, gains, cosine, sine, bias,
            cache,
        )
        returned = exchange_rows(attended, 2)
        returned = returned.transpose(1, 2, 3, 0, 4).reshape(cols * reqs * toks, -1)
        partial = jnp.dot(
            returned, out_weight[0], preferred_element_type=jnp.float32
        ).astype(jnp.bfloat16).reshape(cols, reqs, toks, width)
        mine = lax.dynamic_index_in_dim(partial, col, 0, False)
        other = lax.dynamic_index_in_dim(partial, 1 - col, 0, False)
        other = lax.ppermute(other, "col", [(0, 1), (1, 0)])
        projected = mine.astype(jnp.float32) + other.astype(jnp.float32)
        is_text = (my_positions < TXT)[..., None]
        gate_rows = jnp.where(is_text, modulation[5], modulation[2])
        leaving = (inputs.astype(jnp.float32) + gate_rows * projected).astype(jnp.bfloat16)
        leavings.append(leaving)
        if turn < num_patches + section_count - 2:
            incoming = passed_along(leaving, "section", 1)
    stacked = jnp.stack(leavings)
    mine = lax.dynamic_slice_in_dim(stacked, section, num_patches, 0)
    return mine.transpose(0, 2, 1, 3)[None]


def fits_split(mesh):
    heads = 48 // mesh.shape["col"]
    return mesh.shape["col"] == 2 and heads % (2 * mesh.shape["row"]) == 0


def solution(mesh):
    return jax.shard_map(
        local_split if fits_split(mesh) else local,
        mesh=mesh,
        in_specs=(
            P(None, ("row", "col"), None, None),
            P(),
            P(),
            P(),
            P("section", None, ("row", "col")),
            P("section", None, "col"),
            P("section", "col", None),
            P("section", None, None),
            P("section", None, None, "col", None),
            P("section", ("row", "col"), None, None),
            P(),
        ),
        out_specs=P("section", None, ("row", "col"), None, None),
        check_vma=False,
    )
```

```python
import jax
import jax.numpy as jnp
from jax import lax
from jax.experimental import pallas as pl
from jax.experimental.pallas import tpu as pltpu
from jax.sharding import PartitionSpec as P

HD = 64
TXT = 226
GH = 30
GW = 45
PLEN = 256


def passed_along(value, axis, by):
    size = lax.axis_size(axis)
    pairs = [(i, i + by) for i in range(size) if 0 <= i + by < size]
    return lax.ppermute(value, axis, pairs)


def layer_norm(values, epsilon):
    centered = values - jnp.mean(values, axis=-1, keepdims=True)
    return centered * lax.rsqrt(jnp.mean(centered * centered, axis=-1, keepdims=True) + epsilon)


def rotary_tables(positions):
    video_index = jnp.maximum(positions - TXT, 0)
    is_video = positions >= TXT
    frame_index = video_index // (GH * GW)
    height_index = video_index // GW % GH
    width_index = video_index % GW
    phase_parts = []
    for coordinate, part_size in (
        (frame_index, HD // 4),
        (height_index, HD * 3 // 8),
        (width_index, HD * 3 // 8),
    ):
        frequency = 1.0 / 10000.0 ** (jnp.arange(0, part_size, 2).astype(jnp.float32) / part_size)
        phase_part = coordinate.astype(jnp.float32)[..., None] * frequency
        phase_parts.append(jnp.repeat(phase_part, 2, axis=-1))
    phase_all = jnp.concatenate(phase_parts, axis=-1)
    cosine = jnp.where(is_video[..., None], jnp.cos(phase_all), 1.0)
    sine_table = jnp.where(is_video[..., None], jnp.sin(phase_all), 0.0)
    return (cosine, sine_table)


def rotate_pairs(values, cosine, sine_table):
    paired = values.reshape(values.shape[:-1] + (values.shape[-1] // 2, 2))
    turned = jnp.stack([-paired[..., 1], paired[..., 0]], axis=-1).reshape(values.shape)
    return values * cosine + turned * sine_table


def heads_from(mixed_rows, positions, gain_pair):
    cosine, sine_table = rotary_tables(positions)
    cosine = cosine[..., None, :]
    sine_table = sine_table[..., None, :]
    keys_new = rotate_pairs(
        layer_norm(mixed_rows[..., 1, :], 1e-06) * gain_pair[1], cosine, sine_table
    ).astype(jnp.bfloat16)
    values_new = mixed_rows[..., 2, :].astype(jnp.bfloat16)
    queries = rotate_pairs(
        layer_norm(mixed_rows[..., 0, :], 1e-06) * gain_pair[0], cosine, sine_table
    ).astype(jnp.bfloat16)
    return jnp.concatenate([queries, keys_new, values_new], axis=-1)


def modulate(row_values, positions, modulation):
    is_text = (positions < TXT)[..., None]
    shifts = jnp.where(is_text, modulation[3], modulation[0])
    scales = jnp.where(is_text, modulation[4], modulation[1])
    normed = layer_norm(row_values.astype(jnp.float32), 1e-05)
    return (normed * (1.0 + scales) + shifts).astype(jnp.bfloat16)


def local(
    hidden,
    patch_counts,
    timestep,
    time_table,
    ada_weight,
    qkv_weight,
    out_weight,
    qk_gain,
    stale_kv,
    stale_inputs,
    recompute_slots,
):
    col_count = lax.axis_size("col")
    section_count = lax.axis_size("section")
    section_index = lax.axis_index("section")
    row_index = lax.axis_index("row")
    col_index = lax.axis_index("col")
    num_patches, dev_rows, num_requests, model_width = hidden.shape
    seq_length = PLEN * num_patches
    group_rows = dev_rows * col_count
    starts = jnp.cumsum(patch_counts, axis=1) - patch_counts
    slot_index = jnp.arange(seq_length, dtype=jnp.int32)
    slot_patch = slot_index // PLEN
    slot_offset = slot_index % PLEN
    positions = starts[:, slot_patch] + slot_offset[None, :]
    live_mask = slot_offset[None, :] < patch_counts[:, slot_patch]
    embedding = jax.nn.silu(time_table[timestep[0]]).astype(jnp.bfloat16)
    mod_part = jnp.dot(embedding, ada_weight[0], preferred_element_type=jnp.float32)
    modulation = lax.all_gather(mod_part, ("row", "col"), axis=0, tiled=True).reshape(
        6, model_width
    )
    weights_qkv = qkv_weight[0]
    weights_out = out_weight[0]
    gain_pair = qk_gain[0]
    scale_factor = HD ** (-0.5)

    def project(normed_part, position_table):
        piece_rows = lax.all_gather(normed_part, "col", axis=0, tiled=True)
        mixed_rows = jnp.dot(
            piece_rows.reshape(-1, model_width), weights_qkv, preferred_element_type=jnp.float32
        )
        mixed_rows = mixed_rows.reshape(piece_rows.shape[0], piece_rows.shape[1], -1, 3, HD)
        return heads_from(mixed_rows, position_table, gain_pair)

    def spread_rows(key_value):
        return lax.all_gather(key_value, "row", axis=0, tiled=True)

    rec_dev = stale_inputs.shape[1]
    rec_group = rec_dev * col_count
    rec_positions = jnp.take_along_axis(positions, recompute_slots, axis=1).T
    local_rec = lax.dynamic_slice_in_dim(
        rec_positions, (row_index * col_count + col_index) * rec_dev, rec_dev, 0
    )
    group_rec = lax.dynamic_slice_in_dim(rec_positions, row_index * rec_group, rec_group, 0)
    rec_normed = modulate(stale_inputs[0], local_rec, modulation)
    rec_heads = project(rec_normed, group_rec)
    rec_pairs = spread_rows(rec_heads[..., HD:])
    base_cache = stale_kv[0]
    for request in range(num_requests):
        base_cache = base_cache.at[recompute_slots[request], request].set(rec_pairs[:, request])
    batches = num_requests * num_patches // num_requests
    turn_count = batches + section_count - 1
    local_offsets = (
        row_index * group_rows + col_index * dev_rows + jnp.arange(dev_rows, dtype=jnp.int32)
    )
    group_offsets = row_index * group_rows + jnp.arange(group_rows, dtype=jnp.int32)

    def relay_turn(turn_index, loop_state):
        cache_table, outputs, incoming = loop_state
        batch_index = turn_index - section_index
        is_valid = (batch_index >= 0) & (batch_index < batches)
        clipped = jnp.clip(batch_index, 0, batches - 1)
        first_request = clipped // num_patches * num_requests
        patch_index = clipped % num_patches
        request_starts = starts[:, patch_index]
        local_positions = local_offsets[:, None] + request_starts[None, :]
        group_positions = group_offsets[:, None] + request_starts[None, :]
        entering = hidden[patch_index]
        inputs = jnp.where(section_index == 0, entering, incoming)
        normed = modulate(inputs, local_positions, modulation)
        heads_all = project(normed, group_positions)
        fresh_pairs = spread_rows(heads_all[..., HD:])
        block_start = (patch_index * PLEN, first_request, 0, 0)
        old_block = lax.dynamic_slice(cache_table, block_start, fresh_pairs.shape)
        new_block = jnp.where(is_valid, fresh_pairs, old_block)
        cache_table = lax.dynamic_update_slice(cache_table, new_block, block_start)
        queries = heads_all[..., :HD]
        scores = (
            jnp.einsum(
                "qrhd,krhd->rhqk",
                queries,
                cache_table[..., :HD],
                preferred_element_type=jnp.float32,
            )
            * scale_factor
        )
        weights = jnp.where(live_mask[:, None, None, :], jnp.exp(scores), 0.0)
        totals = jnp.sum(weights, axis=-1)
        attended = jnp.einsum(
            "rhqk,krhd->qrhd",
            weights.astype(jnp.bfloat16),
            cache_table[..., HD:],
            preferred_element_type=jnp.float32,
        )
        attended = (attended / jnp.transpose(totals, (2, 0, 1))[..., None]).astype(jnp.bfloat16)
        flat_rows = attended.reshape(group_rows * num_requests, -1)
        projected = (
            lax.psum_scatter(
                jnp.dot(flat_rows, weights_out, preferred_element_type=jnp.float32).astype(
                    jnp.bfloat16
                ),
                "col",
                scatter_dimension=0,
                tiled=True,
            )
            .astype(jnp.float32)
            .reshape(dev_rows, num_requests, model_width)
        )
        is_text = (local_positions < TXT)[..., None]
        gate_rows = jnp.where(is_text, modulation[5], modulation[2])
        leaving = (inputs.astype(jnp.float32) + gate_rows * projected).astype(jnp.bfloat16)
        out_start = (patch_index, 0, first_request, 0)
        current_out = lax.dynamic_slice(
            outputs, out_start, (1, dev_rows, num_requests, model_width)
        )
        written = jnp.where(is_valid, leaving[None], current_out)
        outputs = lax.dynamic_update_slice(outputs, written, out_start)
        incoming = passed_along(leaving, "section", 1)
        return (cache_table, outputs, incoming)

    outputs_start = jnp.zeros((num_patches, dev_rows, num_requests, model_width), jnp.bfloat16)
    incoming_start = jnp.zeros((dev_rows, num_requests, model_width), jnp.bfloat16)
    final_state = lax.fori_loop(
        0, turn_count, relay_turn, (base_cache, outputs_start, incoming_start)
    )
    return final_state[1][None]


HEAD_PAIR = 6 * HD
DEAD = -1e30


def block_body(patch_ref, cell_ref, x_ref, w_ref, gain_ref, cos_ref, sin_ref, bias_ref, old_ref,
               kv_ref, out_ref):
    cols, rows, reqs, toks, width = x_ref.shape
    total_rows = cols * rows * reqs * toks
    patch = patch_ref[0]
    x = x_ref[...].reshape(total_rows, width)
    mixed = jnp.dot(x, w_ref[0], preferred_element_type=jnp.float32)
    lane = lax.broadcasted_iota(jnp.int32, (total_rows, 2 * HD), 1)
    low = lane < HD
    even = lane % 2 == 0
    cosine = cos_ref[0]
    sine = sin_ref[0]

    def halves_mean(value):
        low_sum = jnp.sum(jnp.where(low, value, 0.0), axis=-1, keepdims=True)
        high_sum = jnp.sum(jnp.where(low, 0.0, value), axis=-1, keepdims=True)
        return jnp.where(low, low_sum, high_sum) * (1.0 / HD)

    def turned(value, gain):
        centered = value - halves_mean(value)
        scaled = centered * lax.rsqrt(halves_mean(centered * centered) + 1e-06) * gain
        swapped = jnp.where(even, pltpu.roll(scaled, 2 * HD - 1, 1), pltpu.roll(scaled, 1, 1))
        return scaled * cosine + swapped * sine

    raw = [mixed[:, i * 2 * HD:(i + 1) * 2 * HD] for i in range(3)]
    done = [turned(raw[i], gain_ref[i:i + 1, :]) for i in range(3)]
    first_kv = jnp.where(low, pltpu.roll(done[0], HD, 1), pltpu.roll(raw[1], HD, 1))
    second_kv = jnp.where(low, done[2], raw[2])
    first_q = jnp.where(low, done[0] * HD ** (-0.5), 0.0)
    second_q = jnp.where(low, pltpu.roll(done[1], HD, 1) * HD ** (-0.5), 0.0)
    pairs = [first_kv.astype(jnp.bfloat16), second_kv.astype(jnp.bfloat16)]
    queries = [first_q.astype(jnp.bfloat16), second_q.astype(jnp.bfloat16)]

    kv_ref[...] = old_ref[...]

    def block_of(c, w, r):
        start = ((c * rows + w) * reqs + r) * toks
        return slice(start, start + toks)

    def plen_of(c, w):
        start = (w * cols + c) * toks
        return slice(start, start + toks)

    for head in range(2):
        for c in range(cols):
            for w in range(rows):
                for r in range(reqs):
                    kv_ref[r, head, patch, plen_of(c, w), :] = pairs[head][block_of(c, w, r), :]
    plen = rows * cols * toks
    low_out = lax.broadcasted_iota(jnp.int32, (plen, 2 * HD), 1) < HD
    for r in range(reqs):
        attended = []
        for head in range(2):
            query = jnp.concatenate(
                [queries[head][block_of(c, w, r), :] for w in range(rows) for c in range(cols)],
                axis=0,
            )
            table = kv_ref[r, head].reshape(-1, 2 * HD)
            scores = lax.dot_general(
                query, table, (((1,), (1,)), ((), ())), preferred_element_type=jnp.float32
            )
            weights = jnp.exp(scores + bias_ref[r:r + 1, :])
            totals = jnp.sum(weights, axis=-1, keepdims=True)
            summed = jnp.dot(
                weights.astype(jnp.bfloat16), table, preferred_element_type=jnp.float32
            )
            attended.append(summed / totals)
        both = jnp.where(low_out, pltpu.roll(attended[0], HD, 1), attended[1])
        both = both.astype(jnp.bfloat16)
        for w in range(rows):
            for c in range(cols):
                out_ref[w, c, r] = both[plen_of(c, w), :]


def block_call(patch, cell, x, weights, gains, cosine, sine, bias, cache):
    cols, rows, reqs, toks, width = x.shape
    pair_count = cache.shape[1] // 2
    patches, plen = cache.shape[2], cache.shape[3]
    total_rows = cols * rows * reqs * toks
    flops = 2 * total_rows * width * HEAD_PAIR * pair_count
    flops += 8 * total_rows * patches * plen * HD * pair_count * 2
    grid_spec = pltpu.PrefetchScalarGridSpec(
        num_scalar_prefetch=2,
        grid=(pair_count,),
        in_specs=[
            pl.BlockSpec(x.shape, lambda j, p, m: (0, 0, 0, 0, 0)),
            pl.BlockSpec((1, width, HEAD_PAIR), lambda j, p, m: (0, 0, m[0] * pair_count + j)),
            pl.BlockSpec(gains.shape, lambda j, p, m: (0, 0)),
            pl.BlockSpec((1, total_rows, 2 * HD), lambda j, p, m: (p[0], 0, 0)),
            pl.BlockSpec((1, total_rows, 2 * HD), lambda j, p, m: (p[0], 0, 0)),
            pl.BlockSpec(bias.shape, lambda j, p, m: (0, 0)),
            pl.BlockSpec((reqs, 2, patches, plen, 2 * HD), lambda j, p, m: (0, j, 0, 0, 0)),
        ],
        out_specs=[
            pl.BlockSpec((reqs, 2, patches, plen, 2 * HD), lambda j, p, m: (0, j, 0, 0, 0)),
            pl.BlockSpec((rows, cols, reqs, toks, 2 * HD), lambda j, p, m: (0, 0, 0, 0, j)),
        ],
    )
    return pl.pallas_call(
        block_body,
        grid_spec=grid_spec,
        out_shape=[
            jax.ShapeDtypeStruct(cache.shape, jnp.bfloat16),
            jax.ShapeDtypeStruct((rows, cols, reqs, toks, pair_count * 2 * HD), jnp.bfloat16),
        ],
        compiler_params=pltpu.CompilerParams(vmem_limit_bytes=44 * 1024 * 1024),
        cost_estimate=pl.CostEstimate(
            flops=flops, bytes_accessed=20 * 1024 * 1024,
            transcendentals=2 * pair_count * total_rows * patches * plen,
        ),
    )(patch, cell, x, weights, gains, cosine, sine, bias, cache)


def modulate_split(values, positions, modulation):
    is_text = (positions < TXT)[..., None]
    shifts = jnp.where(is_text, modulation[3], modulation[0])
    scales = jnp.where(is_text, modulation[4], modulation[1])
    normed = layer_norm(values.astype(jnp.float32), 1e-05)
    return (normed * (1.0 + scales) + shifts).astype(jnp.bfloat16)


def gather_body(x_ref, out_ref, own_sem, line_send, line_recv, far_send, far_recv, side_send,
                side_recv):
    chunks = x_ref.shape[0]
    rows = out_ref.shape[1]
    w = lax.axis_index("row")
    c = lax.axis_index("col")
    above = lax.rem(w + 1, rows)
    below = lax.rem(w + rows - 1, rows)
    across = lax.rem(w + 2, rows)
    barrier = pltpu.get_barrier_semaphore()
    for peer in ({"col": 1 - c}, {"row": above}, {"row": below}):
        pl.semaphore_signal(barrier, inc=1, device_id=peer, device_id_type=pl.DeviceIdType.MESH)
    pl.semaphore_wait(barrier, 3)

    def sent(source, core, block, chunk, send, receive, peer):
        return pltpu.make_async_remote_copy(
            src_ref=source, dst_ref=out_ref.at[core, block, chunk], send_sem=send,
            recv_sem=receive, device_id=peer, device_id_type=pl.DeviceIdType.MESH,
        )

    targets = ({"row": above}, {"row": below})
    arriving = (below, above)

    def near(lane, chunk, block):
        return sent(x_ref.at[chunk], c, block, chunk, line_send.at[lane, chunk],
                    line_recv.at[lane, chunk], targets[lane])

    def far(chunk, block):
        lane = chunk % 2
        return sent(out_ref.at[c, arriving[lane], chunk], c, block, chunk, far_send.at[chunk],
                    far_recv.at[chunk], targets[lane])

    def side(place, chunk, core, block):
        source = x_ref.at[chunk] if place == 0 else out_ref.at[c, block, chunk]
        return sent(source, core, block, chunk, side_send.at[place, chunk],
                    side_recv.at[place, chunk], {"col": 1 - c})

    for first in (0, 1):
        for chunk in range(chunks):
            for lane in (0, 1):
                if (chunk % 2 == lane) == (first == 0):
                    near(lane, chunk, w).start()
    kept = []
    for chunk in range(chunks):
        side(0, chunk, c, w).start()
        copy = pltpu.make_async_copy(x_ref.at[chunk], out_ref.at[c, w, chunk], own_sem.at[chunk])
        copy.start()
        kept.append(copy)
    for chunk in range(chunks):
        lane = chunk % 2
        near(lane, chunk, arriving[lane]).wait_recv()
        far(chunk, arriving[lane]).start()
        side(1 + lane, chunk, c, arriving[lane]).start()
    for chunk in range(chunks):
        lane = 1 - chunk % 2
        near(lane, chunk, arriving[lane]).wait_recv()
        side(1 + lane, chunk, c, arriving[lane]).start()
    for chunk in range(chunks):
        far(chunk, across).wait_recv()
        side(3, chunk, c, across).start()
    for chunk in range(chunks):
        kept[chunk].wait()
        far(chunk, across).wait_send()
        for lane in (0, 1):
            near(lane, chunk, w).wait_send()
        for place, block in enumerate((w, below, above, across)):
            side(place, chunk, c, block).wait_send()
            side(place, chunk, 1 - c, block).wait_recv()


def gather_tokens(value, rows, cols, number):
    chunks = value.shape[0]
    return pl.pallas_call(
        gather_body,
        out_shape=jax.ShapeDtypeStruct((cols, rows) + value.shape, value.dtype),
        in_specs=[pl.BlockSpec(memory_space=pl.ANY)],
        out_specs=pl.BlockSpec(memory_space=pl.ANY),
        scratch_shapes=[
            pltpu.SemaphoreType.DMA((chunks,)),
            pltpu.SemaphoreType.DMA((2, chunks)),
            pltpu.SemaphoreType.DMA((2, chunks)),
            pltpu.SemaphoreType.DMA((chunks,)),
            pltpu.SemaphoreType.DMA((chunks,)),
            pltpu.SemaphoreType.DMA((4, chunks)),
            pltpu.SemaphoreType.DMA((4, chunks)),
        ],
        compiler_params=pltpu.CompilerParams(collective_id=number, has_side_effects=True),
        cost_estimate=pl.CostEstimate(flops=0, bytes_accessed=40 * 1024 * 1024, transcendentals=0),
    )(value)


def project_body(cell_ref, x_ref, w_ref, out_ref):
    out_ref[...] = jnp.dot(x_ref[...], w_ref[0], preferred_element_type=jnp.float32)


def project_call(cell, x, weights, pair_count):
    count, width = x.shape
    return pl.pallas_call(
        project_body,
        grid_spec=pltpu.PrefetchScalarGridSpec(
            num_scalar_prefetch=1,
            grid=(pair_count,),
            in_specs=[
                pl.BlockSpec((count, width), lambda j, m: (0, 0)),
                pl.BlockSpec((1, width, HEAD_PAIR), lambda j, m: (0, 0, m[0] * pair_count + j)),
            ],
            out_specs=pl.BlockSpec((count, HEAD_PAIR), lambda j, m: (0, j)),
        ),
        out_shape=jax.ShapeDtypeStruct((count, HEAD_PAIR * pair_count), jnp.float32),
        compiler_params=pltpu.CompilerParams(vmem_limit_bytes=24 * 1024 * 1024),
    )(cell, x, weights)


def exchange_body(x_ref, out_ref, own_sem, send_sem, recv_sem):
    rows = x_ref.shape[0]
    w = lax.axis_index("row")
    barrier = pltpu.get_barrier_semaphore()
    for way in range(1, rows):
        pl.semaphore_signal(barrier, inc=1, device_id={"row": lax.rem(w + way, rows)},
                            device_id_type=pl.DeviceIdType.MESH)
    pl.semaphore_wait(barrier, rows - 1)
    copies = []
    for way in range(1, rows):
        target = lax.rem(w + way, rows)
        copy = pltpu.make_async_remote_copy(
            src_ref=x_ref.at[target], dst_ref=out_ref.at[w],
            send_sem=send_sem.at[way - 1], recv_sem=recv_sem.at[way - 1],
            device_id={"row": target}, device_id_type=pl.DeviceIdType.MESH,
        )
        copy.start()
        copies.append(copy)
    kept = pltpu.make_async_copy(x_ref.at[w], out_ref.at[w], own_sem)
    kept.start()
    for copy in copies:
        copy.wait()
    kept.wait()


def exchange_rows(value, number):
    rows = value.shape[0]
    return pl.pallas_call(
        exchange_body,
        out_shape=jax.ShapeDtypeStruct(value.shape, value.dtype),
        in_specs=[pl.BlockSpec(memory_space=pl.ANY)],
        out_specs=pl.BlockSpec(memory_space=pl.ANY),
        scratch_shapes=[
            pltpu.SemaphoreType.DMA,
            pltpu.SemaphoreType.DMA((rows - 1,)),
            pltpu.SemaphoreType.DMA((rows - 1,)),
        ],
        compiler_params=pltpu.CompilerParams(collective_id=number, has_side_effects=True),
        cost_estimate=pl.CostEstimate(flops=0, bytes_accessed=16 * 1024 * 1024, transcendentals=0),
    )(value)


def local_split(
    hidden,
    patch_counts,
    timestep,
    time_table,
    ada_weight,
    qkv_weight,
    out_weight,
    qk_gain,
    stale_kv,
    stale_inputs,
    recompute_slots,
):
    cols = lax.axis_size("col")
    rows = lax.axis_size("row")
    section_count = lax.axis_size("section")
    section = lax.axis_index("section")
    row = lax.axis_index("row")
    col = lax.axis_index("col")
    num_patches, toks, reqs, width = hidden.shape
    seq = PLEN * num_patches
    heads_here = stale_kv.shape[3] // rows
    starts = jnp.cumsum(patch_counts, axis=1) - patch_counts
    slots = jnp.arange(seq, dtype=jnp.int32)
    positions = starts[:, slots // PLEN] + slots[None, :] % PLEN
    live = slots[None, :] % PLEN < patch_counts[:, slots // PLEN]
    bias = jnp.where(live, 0.0, DEAD).astype(jnp.float32)

    embedding = jax.nn.silu(time_table[timestep[0]]).astype(jnp.bfloat16)
    mod_part = jnp.dot(embedding, ada_weight[0], preferred_element_type=jnp.float32)
    mod_all = gather_tokens(jnp.broadcast_to(mod_part, (1, 8) + mod_part.shape), rows, cols, 3)
    modulation = mod_all[:, :, 0, 0].transpose(1, 0, 2).reshape(6, width)

    cell_positions = positions.reshape(reqs, num_patches, rows, cols, toks)
    cell_positions = cell_positions.transpose(1, 3, 2, 0, 4).reshape(num_patches, -1)
    cosine, sine = rotary_tables(cell_positions)
    signs = jnp.where(jnp.arange(HD) % 2 == 0, -1.0, 1.0)
    sine = sine * signs
    cosine = jnp.concatenate([cosine, cosine], axis=-1)
    sine = jnp.concatenate([sine, sine], axis=-1)
    gain_q, gain_k = qk_gain[0, 0], qk_gain[0, 1]
    ones = jnp.ones_like(gain_q)
    gains = jnp.stack([
        jnp.concatenate([gain_q, gain_k]),
        jnp.concatenate([ones, gain_q]),
        jnp.concatenate([gain_k, ones]),
    ])

    rec = recompute_slots.shape[1]
    rec_toks = rec // (rows * cols)
    rec_positions = jnp.take_along_axis(positions, recompute_slots, axis=1)
    my_rec = lax.dynamic_slice_in_dim(rec_positions, (row * cols + col) * rec_toks, rec_toks, 1)
    rec_normed = modulate_split(stale_inputs[0], my_rec.T, modulation)
    entering = hidden.transpose(0, 2, 1, 3)
    my_offsets = (row * cols + col) * toks + jnp.arange(toks, dtype=jnp.int32)
    rec_part = rec_normed.reshape(rec_toks * reqs, width)
    padded = -(-rec_toks * reqs // toks) * toks
    rec_part = jnp.pad(rec_part, ((0, padded - rec_toks * reqs), (0, 0)))
    first_positions = starts[:, 0][:, None] + my_offsets[None, :]
    first_normed = modulate_split(entering[0], first_positions, modulation)
    first_all = gather_tokens(
        jnp.concatenate([first_normed, rec_part.reshape(-1, toks, width)], axis=0), rows, cols, 0
    )
    rec_all = first_all[:, :, reqs:].reshape(cols, rows, padded, width)
    rec_all = rec_all[:, :, :rec_toks * reqs]

    def by_cell(table):
        table = table.reshape(reqs, rows, cols, rec_toks).transpose(2, 1, 3, 0)
        return table.reshape(-1, reqs)

    rec_places = by_cell(rec_positions)
    rec_slots = by_cell(recompute_slots)
    cell = jnp.reshape(row, (1,)).astype(jnp.int32)
    rec_mixed = project_call(cell, rec_all.reshape(-1, width), qkv_weight, heads_here // 2)
    rec_mixed = rec_mixed.reshape(rec, reqs, heads_here, 3, HD)
    rec_pairs = heads_from(rec_mixed, rec_places, qk_gain[0])[..., HD:]
    stale_here = lax.dynamic_slice_in_dim(stale_kv[0], row * heads_here, heads_here, 2)
    stale_here = stale_here.transpose(1, 2, 0, 3)
    match = (slots[None, :, None] == rec_slots.T[:, None, :])
    placed = jnp.einsum(
        "rsi,irhd->rhsd", match.astype(jnp.bfloat16), rec_pairs,
        preferred_element_type=jnp.float32,
    ).astype(jnp.bfloat16)
    replaced = jnp.any(match, axis=-1)[:, None, :, None]
    cache = jnp.where(replaced, placed, stale_here)
    cache = cache.reshape(reqs, heads_here, num_patches, PLEN, 2 * HD)

    leavings = []
    incoming = entering[0]
    for turn in range(num_patches + section_count - 1):
        patch = jnp.clip(turn - section, 0, num_patches - 1).astype(jnp.int32)
        my_positions = starts[:, patch][:, None] + my_offsets[None, :]
        if turn == 0 or turn >= num_patches:
            inputs = incoming
        else:
            inputs = jnp.where(section == 0, entering[turn], incoming)
        if turn == 0:
            tokens = first_all[:, :, :reqs]
        else:
            normed = modulate_split(inputs, my_positions, modulation)
            tokens = gather_tokens(normed, rows, cols, 1)
        cache, attended = block_call(
            patch.reshape(1), cell, tokens, qkv_weight, gains, cosine, sine, bias,
            cache,
        )
        returned = exchange_rows(attended, 2)
        returned = returned.transpose(1, 2, 3, 0, 4).reshape(cols * reqs * toks, -1)
        partial = jnp.dot(
            returned, out_weight[0], preferred_element_type=jnp.float32
        ).astype(jnp.bfloat16).reshape(cols, reqs, toks, width)
        mine = lax.dynamic_index_in_dim(partial, col, 0, False)
        other = lax.dynamic_index_in_dim(partial, 1 - col, 0, False)
        other = lax.ppermute(other, "col", [(0, 1), (1, 0)])
        projected = mine.astype(jnp.float32) + other.astype(jnp.float32)
        is_text = (my_positions < TXT)[..., None]
        gate_rows = jnp.where(is_text, modulation[5], modulation[2])
        leaving = (inputs.astype(jnp.float32) + gate_rows * projected).astype(jnp.bfloat16)
        leavings.append(leaving)
        if turn < num_patches + section_count - 2:
            incoming = passed_along(leaving, "section", 1)
    stacked = jnp.stack(leavings)
    mine = lax.dynamic_slice_in_dim(stacked, section, num_patches, 0)
    return mine.transpose(0, 2, 1, 3)[None]


def fits_split(mesh):
    heads = 48 // mesh.shape["col"]
    return mesh.shape["col"] == 2 and mesh.shape["row"] == 4 and heads % (2 * mesh.shape["row"]) == 0


def solution(mesh):
    return jax.shard_map(
        local_split if fits_split(mesh) else local,
        mesh=mesh,
        in_specs=(
            P(None, ("row", "col"), None, None),
            P(),
            P(),
            P(),
            P("section", None, ("row", "col")),
            P("section", None, "col"),
            P("section", "col", None),
            P("section", None, None),
            P("section", None, None, "col", None),
            P("section", ("row", "col"), None, None),
            P(),
        ),
        out_specs=P("section", None, ("row", "col"), None, None),
        check_vma=False,
    )
```
